128 devices in a mesh: seq: 16 (over z, y_hi, core), head: 8 (over y_lo, x).
Axes of the slice: x: 4, y: 4 (y_hi: 2, y_lo: 2; y = y_hi * 2 + y_lo), z: 4, core: 2. Of those that a mesh axis runs over, the one named last changes fastest.
Arguments:
- queries: bfloat16 [8192, 8192], P('seq', 'head'), may hold values from -7 to 7
- key_states: bfloat16 [8192, 1024], P(('seq', 'head')), may hold values from -6 to 6
- value_states: bfloat16 [8192, 1024], P(('seq', 'head')), may hold values from -6 to 6
- passing_rows: int32 [8, 4096], P('head', 'seq'), may hold values from 0 to 511, as said below
Outputs:
- attended: bfloat16 [8192, 8192], P('seq', 'head')
The draws below stay inside these ranges and needn't reach their ends.
Inputs may be any that keep to these rules, and one draw needn't show every extreme that they name: `passing_rows`: for each KV head and each block the 256 entries are distinct, in increasing order, and include 0 and 511.
All inputs are finite; a program needn't handle non-finite values.
Results may differ from the reference program's by a relative error of at most 0.009.
Values may be sent and summed in bfloat16 or wider, within the bound.
No kernel may reach another device: no remote copies, remote signals or barrier semaphores. Data moves between devices by JAX's collectives and lax.ppermute only.
A program may use at most 320 MiB of HBM per device.

```python
import jax
import jax.numpy as jnp
from jax import lax

QH = 64
KVH = 8
HD = 128
BLK = 512
PASS = 256
ANCHOR = 256
TOKENS = 8192


def draw_queries(key, part):
    key = jax.random.fold_in(key, 11)
    result = jax.random.truncated_normal(key, -6.0, 6.0, (TOKENS, QH, HD), jnp.float32)
    return result.reshape(TOKENS, QH * HD).astype(jnp.bfloat16)


def draw_key_states(key, part):
    key = jax.random.fold_in(key, 12)
    result = jax.random.truncated_normal(key, -6.0, 6.0, (TOKENS, KVH * HD), jnp.float32)
    return result.astype(jnp.bfloat16)


def draw_passing_rows(key, part):
    key = jax.random.fold_in(key, 13)
    blocks = TOKENS // BLK
    group_keys = jax.random.split(key, KVH * blocks)

    def one_group(group_key):
        middle_rows = (jax.random.permutation(group_key, BLK - 2)[:PASS - 2] + 1).astype(jnp.int32)
        joined = jnp.concatenate([jnp.zeros((1,), jnp.int32), middle_rows, jnp.full((1,), BLK - 1, jnp.int32)])
        return jnp.sort(joined)
    return jax.vmap(one_group)(group_keys).reshape(KVH, blocks * PASS)


def shard_levels(stream_key, extent, cuts, smallest, top_value):
    def one(axis_at, blocks):
        steps = jax.random.uniform(jax.random.fold_in(jax.random.fold_in(stream_key, 6), axis_at), (blocks,), jnp.float32, smallest / len(cuts), top_value / len(cuts))
        return jnp.repeat(jnp.exp(steps), extent[axis_at] // blocks).reshape((-1,) + (1,) * (len(extent) - axis_at - 1))

    level = one(*cuts[0])
    for cut in cuts[1:]:
        level = level * one(*cut)
    return level


def normal_values(stream_key, dims, spread, most, cuts=(), kind=jnp.bfloat16):
    drawn = jax.random.normal(stream_key, dims, jnp.float32) * spread
    if len(cuts) > 0:
        drawn = shard_levels(stream_key, dims, cuts, -0.22, 0.18) * drawn
    return jnp.clip(drawn, min=-most, max=most).astype(kind)


def setup_inputs(seed: int = 0) -> dict:
    key_of = jax.random.split(jax.random.key(seed), 5)
    queries = draw_queries(jax.random.fold_in(key_of[4], 71), 0)
    key_states = draw_key_states(jax.random.fold_in(key_of[4], 71), 0)
    value_states = normal_values(key_of[2], (TOKENS, KVH * HD), 1.0, 6.0, ((0, 128),))
    passing_rows = draw_passing_rows(jax.random.fold_in(key_of[4], 71), 0)
    return dict(queries=queries, key_states=key_states, value_states=value_states, passing_rows=passing_rows)


def reference(queries, key_states, value_states, passing_rows):
    blocks = TOKENS // BLK
    group_size = QH // KVH
    score_scale = HD ** -0.5
    keys_all = key_states.reshape(TOKENS, KVH, HD)
    values_all = value_states.reshape(TOKENS, KVH, HD)
    query_all = queries.reshape(blocks, BLK, KVH, group_size, HD)
    owner_host = (jnp.arange(blocks * PASS) // PASS).astype(jnp.int32)
    causal = (jnp.arange(BLK)[None, :] <= jnp.arange(BLK)[:, None])[:, None, :]

    def per_head(head_id):
        head_keys = lax.dynamic_index_in_dim(keys_all, head_id, 1, keepdims=False)
        head_values = lax.dynamic_index_in_dim(values_all, head_id, 1, keepdims=False)
        row_ids = lax.dynamic_index_in_dim(passing_rows, head_id, 0, keepdims=False).astype(jnp.int32) + owner_host * BLK
        pass_keys = head_keys[row_ids]
        pass_values = head_values[row_ids]

        def per_block(block_id):
            block_all = lax.dynamic_index_in_dim(query_all, block_id, 0, keepdims=False)
            block_queries = lax.dynamic_index_in_dim(block_all, head_id, 1, keepdims=False)
            start_row = (block_id * BLK).astype(jnp.int32)
            local_keys = lax.dynamic_slice_in_dim(head_keys, start_row, BLK, 0)
            local_values = lax.dynamic_slice_in_dim(head_values, start_row, BLK, 0)
            all_keys = jnp.concatenate([head_keys[:ANCHOR], pass_keys, local_keys], 0)
            all_values = jnp.concatenate([head_values[:ANCHOR], pass_values, local_values], 0)
            usable = jnp.concatenate([
                jnp.broadcast_to(block_id >= 1, (BLK, 1, ANCHOR)),
                jnp.broadcast_to((owner_host < block_id)[None, None, :], (BLK, 1, blocks * PASS)),
                causal], 2)
            scores = jnp.einsum('trd,cd->trc', block_queries.astype(jnp.float32), all_keys.astype(jnp.float32)) * score_scale
            row_max = jnp.max(jnp.where(usable, scores, -jnp.inf), axis=-1, keepdims=True)
            exps = jnp.exp(jnp.where(usable, scores - row_max, -jnp.inf))
            totals = jnp.sum(exps, axis=-1, keepdims=True)
            weights = exps.astype(jnp.bfloat16)
            mixed = jnp.einsum('trc,cd->trd', weights.astype(jnp.float32), all_values.astype(jnp.float32))
            return (mixed / totals).astype(jnp.bfloat16)

        return lax.map(per_block, jnp.arange(blocks, dtype=jnp.int32))

    result = lax.map(per_head, jnp.arange(KVH, dtype=jnp.int32))
    return jnp.transpose(result, (1, 2, 0, 3, 4)).reshape(TOKENS, QH * HD)
```

```python
import functools

import jax
import jax.numpy as jnp
from jax import lax
from jax.experimental import pallas as pl
from jax.experimental.pallas import tpu as pltpu
from jax.sharding import PartitionSpec as P

HD = 128
GROUP = 8
BLK = 512
PASS = 256
ANCHOR = 256
SCALE = float(HD**-0.5 * 1.4426950408889634)
LIMIT = 1e30
BF16, F32 = jnp.bfloat16, jnp.float32
NT = (((1,), (1,)), ((), ()))
VMEM_BYTES = 40 * 2**20
UNROLL = 2


def full(count):
    return [pl.BlockSpec(memory_space=pltpu.VMEM)] * count


def cost(units):
    return pl.CostEstimate(
        flops=int(units * 2 * 2 * GROUP * BLK * 256 * 256),
        bytes_accessed=1 << 20,
        transcendentals=int(units * GROUP * BLK * 256),
    )


def params():
    return pltpu.CompilerParams(vmem_limit_bytes=VMEM_BYTES)


def select_kernel(rows_ref, kv_ref, out_ref):
    rows = rows_ref[...]
    ids = lax.broadcasted_iota(jnp.int32, (BLK, PASS), 0)
    picked = jnp.where(ids == rows, 1.0, 0.0).astype(BF16)
    out_ref[...] = lax.dot_general(
        picked, kv_ref[...], (((0,), (0,)), ((), ())), preferred_element_type=F32
    ).astype(BF16)


def select(rows, kv):
    return pl.pallas_call(
        select_kernel,
        out_shape=jax.ShapeDtypeStruct((PASS, 2 * HD), BF16),
        in_specs=full(2),
        out_specs=pl.BlockSpec(memory_space=pltpu.VMEM),
        compiler_params=params(),
        name="select_rows",
    )(rows, kv)


def widen(wide, at, kv):
    count = kv.shape[0]
    wide[at : at + count, :HD] = kv[:, HD:]
    wide[at : at + count, HD:] = jnp.ones((count, HD), BF16)


def powers(scores, shift):
    parts = [
        jnp.exp2(scores[:, j : j + HD] * SCALE - shift) for j in range(0, scores.shape[1], HD)
    ]
    return jnp.concatenate([part.astype(BF16) for part in parts], axis=1)


def heads(body):
    def step(r, carry):
        body(r)
        return carry

    lax.fori_loop(0, GROUP, step, 0, unroll=UNROLL)


def columns(r):
    return pl.ds(pl.multiple_of(r * HD, HD), HD)


def local_kernel(q_ref, kv_ref, acc_ref, shift_ref, wide):
    widen(wide, 0, kv_ref[...])
    half = BLK // 2
    ones = jnp.ones((HD, HD), BF16)
    rows = lax.broadcasted_iota(jnp.int32, (half, half), 0)
    cols = lax.broadcasted_iota(jnp.int32, (half, half), 1)
    causal = cols <= rows

    def body(r):
        q = q_ref[:, columns(r)]
        k = kv_ref[:, :HD]
        own = (q.astype(F32) * k.astype(F32)).astype(BF16)
        shift = jnp.dot(own, ones, preferred_element_type=F32) * SCALE
        shift_ref[r] = shift
        for t in range(2):
            tile = slice(t * half, (t + 1) * half)
            weights = []
            for u in range(t + 1):
                scores = lax.dot_general(
                    q[tile], k[u * half : (u + 1) * half], NT, preferred_element_type=F32
                )
                if u == t:
                    scores = jnp.where(causal, scores, -jnp.inf)
                weights.append(powers(scores, shift[tile]))
            weights = jnp.concatenate(weights, axis=1)
            acc_ref[r, tile] = jnp.dot(
                weights, wide[: (t + 1) * half], preferred_element_type=F32
            )

    heads(body)


def local_part(q, kv):
    return pl.pallas_call(
        local_kernel,
        out_shape=(
            jax.ShapeDtypeStruct((GROUP, BLK, 2 * HD), F32),
            jax.ShapeDtypeStruct((GROUP, BLK, HD), F32),
        ),
        in_specs=full(2),
        out_specs=tuple(full(2)),
        scratch_shapes=[pltpu.VMEM((BLK, 2 * HD), BF16)],
        compiler_params=params(),
        cost_estimate=cost(1.5),
        name="local_block",
    )(q, kv)


def add_keys(q_ref, acc_ref, shift_ref, refs, keys, wide):
    at = 0
    for ref in refs:
        kv = ref[...]
        keys[at : at + kv.shape[0]] = kv[:, :HD]
        widen(wide, at, kv)
        at += kv.shape[0]

    def body(r):
        scores = lax.dot_general(
            q_ref[:, columns(r)], keys[:at], NT, preferred_element_type=F32
        )
        weights = powers(scores, shift_ref[r])
        acc_ref[r] += jnp.dot(weights, wide[:at], preferred_element_type=F32)

    heads(body)


def stage_kernel(groups, use_ref, q_ref, shift_ref, *refs):
    count = sum(groups)
    kv_refs, (_, acc_ref, keys, wide) = refs[:count], refs[count:]
    at = 0
    for g, size in enumerate(groups):
        members = kv_refs[at : at + size]
        at += size

        @pl.when(use_ref[g] != 0)
        def _():
            add_keys(q_ref, acc_ref, shift_ref, members, keys, wide)


def stage(use, q, shift, acc, groups):
    flat = [x for group in groups for x in group]
    rows = max(sum(x.shape[0] for x in group) for group in groups)
    units = sum(x.shape[0] for x in flat) / 256
    return pl.pallas_call(
        functools.partial(stage_kernel, [len(group) for group in groups]),
        out_shape=jax.ShapeDtypeStruct(acc.shape, F32),
        in_specs=[pl.BlockSpec(memory_space=pltpu.SMEM)] + full(3 + len(flat)),
        out_specs=pl.BlockSpec(memory_space=pltpu.VMEM),
        scratch_shapes=[pltpu.VMEM((rows, HD), BF16), pltpu.VMEM((rows, 2 * HD), BF16)],
        input_output_aliases={3 + len(flat): 0},
        compiler_params=params(),
        cost_estimate=cost(units),
        name="add_blocks",
    )(use, q, shift, *flat, acc)


def online(q, keys, values, usable, running):
    top, total, mixed = running
    scores = lax.dot_general(q, keys, NT, preferred_element_type=F32) * SCALE
    if usable is not None:
        scores = jnp.where(usable, scores, -jnp.inf)
    fresh = jnp.maximum(top, jnp.max(scores, axis=1, keepdims=True))
    rescale = jnp.exp2(top - fresh)
    weights = jnp.exp2(scores - fresh)
    total = total * rescale + jnp.sum(weights, axis=1, keepdims=True)
    mixed = mixed * rescale + jnp.dot(weights.astype(BF16), values, preferred_element_type=F32)
    return fresh, total, mixed


def final_kernel(groups, stages, use_ref, q_ref, shift_ref, *refs):
    count = sum(groups)
    kv_refs, (local_ref, acc_in, out_ref, acc_ref, keys, wide, worst) = refs[:count], refs[count:]
    acc_ref[...] = acc_in[...]
    at = 0
    for g, size in enumerate(groups):
        members = kv_refs[at : at + size]
        at += size
        if g not in stages:
            continue

        @pl.when(use_ref[g] != 0)
        def _():
            add_keys(q_ref, acc_ref, shift_ref, members, keys, wide)

    worst[...] = jnp.zeros_like(worst)

    def finish(r):
        total = acc_ref[r, :, HD:]
        worst[...] = jnp.maximum(worst[...], jnp.where(total < LIMIT, 0.0, 1.0))
        out_ref[:, columns(r)] = (acc_ref[r, :, :HD] / total).astype(BF16)

    heads(finish)

    @pl.when(jnp.max(worst[...]) > 0.0)
    def _():
        tile = 128

        def redo(step, carry):
            r, t = step // (BLK // tile), step % (BLK // tile)
            here = pl.ds(pl.multiple_of(t * tile, tile), tile)
            q = q_ref[here, columns(r)]
            running = (
                jnp.full((tile, 1), -1e30, F32),
                jnp.zeros((tile, 1), F32),
                jnp.zeros((tile, HD), F32),
            )
            rows = t * tile + lax.broadcasted_iota(jnp.int32, (tile, BLK), 0)
            cols = lax.broadcasted_iota(jnp.int32, (tile, BLK), 1)
            running = online(q, local_ref[:, :HD], local_ref[:, HD:], cols <= rows, running)
            at = 0
            for g, size in enumerate(groups):
                for ref in kv_refs[at : at + size]:
                    running = lax.cond(
                        use_ref[g] != 0,
                        lambda s, ref=ref: online(q, ref[:, :HD], ref[:, HD:], None, s),
                        lambda s: s,
                        running,
                    )
                at += size
            out_ref[here, columns(r)] = (running[2] / running[1]).astype(BF16)
            return carry

        lax.fori_loop(0, GROUP * (BLK // tile), redo, 0)


def final(use, q, shift, acc, local_kv, groups, stages):
    flat = [x for group in groups for x in group]
    sizes = [sum(x.shape[0] for x in group) for group in groups]
    rows = max(sizes[g] for g in stages)
    units = sum(sizes[g] for g in stages) / 256
    return pl.pallas_call(
        functools.partial(final_kernel, [len(group) for group in groups], tuple(stages)),
        out_shape=jax.ShapeDtypeStruct((BLK, GROUP * HD), BF16),
        in_specs=[pl.BlockSpec(memory_space=pltpu.SMEM)] + full(4 + len(flat)),
        out_specs=pl.BlockSpec(memory_space=pltpu.VMEM),
        scratch_shapes=[
            pltpu.VMEM(acc.shape, F32),
            pltpu.VMEM((rows, HD), BF16),
            pltpu.VMEM((rows, 2 * HD), BF16),
            pltpu.VMEM((BLK, HD), F32),
        ],
        compiler_params=params(),
        cost_estimate=cost(units),
        name="last_blocks",
    )(use, q, shift, *flat, local_kv, acc)


def place(z, h, c):
    return 4 * z + 2 * h + c


SIBLING = [(s, s ^ 1) for s in range(16)]
PEER = [(s, s ^ 2) for s in range(16)]


def ahead(d):
    return [(s, s + 4 * d) for s in range(16 - 4 * d)]


def local(queries, key_states, value_states, passing_rows):
    me = lax.axis_index("seq")
    z, h, c = me // 4, (me // 2) % 2, me % 2
    move = functools.partial(lax.ppermute, axis_name="seq")

    heads_all = key_states.shape[1] // HD
    rows = key_states.shape[0]
    both = jnp.concatenate(
        [key_states.reshape(rows, heads_all, HD), value_states.reshape(rows, heads_all, HD)], axis=2
    ).transpose(1, 0, 2)
    kv = lax.all_to_all(both, "head", split_axis=0, concat_axis=0, tiled=True).reshape(BLK, 2 * HD)

    mine = select(passing_rows, kv)
    peer = move(mine, perm=PEER)
    acc, shift = local_part(queries, kv)

    anchor = kv[:ANCHOR]
    anchor_peer = move(anchor, perm=[(place(0, 0, 0), place(0, 1, 0))])
    anchor = jnp.where(me == place(0, 1, 0), anchor_peer, anchor)
    anchor_side = move(anchor, perm=[(place(0, 0, 0), place(0, 0, 1)), (place(0, 1, 0), place(0, 1, 1))])
    anchor = jnp.where((z == 0) & (c == 1), anchor_side, anchor)
    onward = move(
        anchor,
        perm=[(place(0, y, 0), place(1, y, 0)) for y in range(2)]
        + [(place(0, y, 1), place(2, y, 1)) for y in range(2)],
    )
    onward_side = move(
        onward,
        perm=[(place(1, y, 0), place(1, y, 1)) for y in range(2)]
        + [(place(2, y, 1), place(2, y, 0)) for y in range(2)],
    )
    half = jnp.where(c == 0, anchor[: ANCHOR // 2], anchor[ANCHOR // 2 :])

    pair = jnp.concatenate([mine, peer], axis=0)
    one = move(pair, perm=ahead(1))
    three = move(jnp.concatenate([pair, half], axis=0), perm=ahead(3))
    two = move(pair, perm=ahead(2))
    pair_side = move(pair, perm=SIBLING)
    one_side = move(one, perm=SIBLING)
    three_side = move(three, perm=SIBLING)
    two_side = move(two, perm=SIBLING)

    relayed = jnp.where(z == 0, anchor, jnp.where(((z == 1) & (c == 0)) | ((z == 2) & (c == 1)), onward, onward_side))

    def flags(*conditions):
        return jnp.stack([jnp.asarray(x).astype(jnp.int32) for x in conditions])

    near = [[peer, pair_side[PASS:]], [pair_side[:PASS]]]
    near_use = [h == 1, c == 1]
    acc = stage(flags(*near_use), queries, shift, acc, near)
    first = [[one, one_side]]
    acc = stage(flags(z >= 1), queries, shift, acc, first)
    rest = [[three, three_side], [relayed], [two, two_side]]
    rest_use = [z == 3, (me >= 1) & (z < 3), z >= 2]
    return final(
        flags(*(near_use + [z >= 1] + rest_use)),
        queries, shift, acc, kv, near + first + rest, [3, 4, 5],
    )


def solution(mesh):
    in_specs = (
        P("seq", "head"),
        P(("seq", "head"), None),
        P(("seq", "head"), None),
        P("head", "seq"),
    )
    return jax.shard_map(
        local, mesh=mesh, in_specs=in_specs, out_specs=P("seq", "head"), check_vma=False
    )
```

```python
import functools

import jax
import jax.numpy as jnp
from jax import lax
from jax.experimental import pallas as pl
from jax.experimental.pallas import tpu as pltpu
from jax.sharding import PartitionSpec as P

HD = 128
GROUP = 8
BLK = 512
PASS = 256
HALF = 128
SCALE = float(HD**-0.5 * 1.4426950408889634)
LOW, HIGH = 2.0**-80, 2.0**100
BF16, F32 = jnp.bfloat16, jnp.float32
NT = (((1,), (1,)), ((), ()))
VMEM_BYTES = 24 * 2**20
SMEM = pl.BlockSpec(memory_space=pltpu.SMEM)
VMEM = pl.BlockSpec(memory_space=pltpu.VMEM)


TOKEN = jax.ShapeDtypeStruct((8, HD), F32)


def cost(units):
    return pl.CostEstimate(
        flops=int(units * 2 * 2 * GROUP * BLK * 256 * 256),
        bytes_accessed=1 << 20,
        transcendentals=int(units * GROUP * BLK * 256),
    )


def params():
    return pltpu.CompilerParams(vmem_limit_bytes=VMEM_BYTES)


def columns(r):
    return slice(r * HD, (r + 1) * HD)


def select_kernel(core_ref, rows_ref, kv_ref, side_ref, out_ref):
    rows = rows_ref[...]
    ids = lax.broadcasted_iota(jnp.int32, (BLK, PASS), 0)
    picked = jnp.where(ids == rows, 1.0, 0.0).astype(BF16)
    out_ref[:PASS] = lax.dot_general(
        picked, kv_ref[...], (((0,), (0,)), ((), ())), preferred_element_type=F32
    ).astype(BF16)

    @pl.when(core_ref[0] == 0)
    def _():
        out_ref[PASS:] = kv_ref[:HALF]

    @pl.when(core_ref[0] != 0)
    def _():
        out_ref[PASS:] = side_ref[HALF : 2 * HALF]


def select(core, rows, kv, side):
    return pl.pallas_call(
        select_kernel,
        out_shape=jax.ShapeDtypeStruct((PASS + HALF, 2 * HD), BF16),
        in_specs=[SMEM, VMEM, VMEM, VMEM],
        out_specs=VMEM,
        compiler_params=params(),
        name="select_rows",
    )(core, rows, kv, side)


def join_kernel(half_ref, mine_ref, peer_ref, out_ref):
    out_ref[:PASS] = mine_ref[:PASS]
    out_ref[PASS : 2 * PASS] = peer_ref[:PASS]

    @pl.when(half_ref[0] == 0)
    def _():
        out_ref[2 * PASS :] = mine_ref[PASS:]

    @pl.when(half_ref[0] != 0)
    def _():
        out_ref[2 * PASS :] = peer_ref[PASS:]


def join(half, mine, peer):
    return pl.pallas_call(
        join_kernel,
        out_shape=jax.ShapeDtypeStruct((2 * PASS + HALF, 2 * HD), BF16),
        in_specs=[SMEM, VMEM, VMEM],
        out_specs=VMEM,
        compiler_params=params(),
        name="join_rows",
    )(half, mine, peer)


def powers(scores):
    return jnp.exp2(scores * SCALE).astype(BF16)


def first_kernel(groups, use_ref, q_ref, kv_ref, *refs):
    near_refs, (acc_ref, token_ref, keys_near, wide) = refs[:-4], refs[-4:]
    token_ref[...] = jnp.zeros_like(token_ref)
    wide[:BLK, :HD] = kv_ref[:, HD:]
    wide[:BLK, HD:] = jnp.ones((BLK, HD), BF16)
    half = BLK // 2
    rows = lax.broadcasted_iota(jnp.int32, (half, half), 0)
    cols = lax.broadcasted_iota(jnp.int32, (half, half), 1)
    causal = cols <= rows
    keys = kv_ref[:, :HD]

    for r in range(GROUP):
        q = q_ref[:, columns(r)]
        scores = lax.dot_general(q, keys[:half], NT, preferred_element_type=F32)
        first = powers(jnp.where(causal, scores[:half], -jnp.inf))
        second = powers(scores[half:])
        scores = lax.dot_general(q[half:], keys[half:], NT, preferred_element_type=F32)
        third = powers(jnp.where(causal, scores, -jnp.inf))
        acc_ref[r, :half] = jnp.dot(first, wide[:half], preferred_element_type=F32)
        acc_ref[r, half:] = jnp.dot(
            jnp.concatenate([second, third], axis=1), wide[:BLK], preferred_element_type=F32
        )

    def put(r, across, total):
        acc_ref[r] = total

    run_groups(groups, use_ref, q_ref, acc_ref, near_refs, keys_near, wide, put)


def first_part(use, q, kv, arrays, groups):
    rows = max(BLK, *[rows_of(case) for _, case, _ in groups])
    return pl.pallas_call(
        functools.partial(first_kernel, groups),
        out_shape=(jax.ShapeDtypeStruct((GROUP, BLK, 2 * HD), F32), TOKEN),
        in_specs=[SMEM] + [VMEM] * (2 + len(arrays)),
        out_specs=(VMEM, VMEM),
        scratch_shapes=[pltpu.VMEM((rows, HD), BF16), pltpu.VMEM((rows, 2 * HD), BF16)],
        compiler_params=params(),
        cost_estimate=cost(4.5),
        name="first_blocks",
    )(use, q, kv, *arrays)


def rows_of(case):
    return sum(stop - start for _, start, stop in case)


def heads(body, unroll):
    if unroll == GROUP:
        for r in range(GROUP):
            body(r, columns(r))
        return

    def step(r, carry):
        body(r, pl.ds(pl.multiple_of(r * HD, HD), HD))
        return carry

    lax.fori_loop(0, GROUP, step, 0, unroll=unroll)


def weighted(case, unroll, q_ref, acc_ref, kv_refs, keys, wide, put):
    at = 0
    for i, start, stop in case:
        end = at + stop - start
        keys[at:end] = kv_refs[i][start:stop, :HD]
        wide[at:end, :HD] = kv_refs[i][start:stop, HD:]
        wide[at:end, HD:] = jnp.ones((end - at, HD), BF16)
        at = end

    def body(r, across):
        scores = lax.dot_general(q_ref[:, across], keys[:at], NT, preferred_element_type=F32)
        put(r, across, acc_ref[r] + jnp.dot(powers(scores), wide[:at], preferred_element_type=F32))

    heads(body, unroll)


def run_groups(groups, use_ref, q_ref, acc_ref, kv_refs, keys, wide, put):
    for flag, case, unroll in groups:

        @pl.when(use_ref[flag] != 0)
        def _():
            weighted(case, unroll, q_ref, acc_ref, kv_refs, keys, wide, put)


def hand_over(use_ref, flag, acc_ref, put):
    @pl.when(use_ref[flag] != 0)
    def _():
        heads(lambda r, across: put(r, across, acc_ref[r]), 1)


def stage_kernel(fresh, more, idle, use_ref, q_ref, *refs):
    kv_refs, (acc_in, acc_ref, token_ref, keys, wide) = refs[:-5], refs[-5:]
    token_ref[...] = jnp.zeros_like(token_ref)

    def put(r, across, total):
        acc_ref[r] = total

    hand_over(use_ref, idle, acc_in, put)
    run_groups(fresh, use_ref, q_ref, acc_in, kv_refs, keys, wide, put)
    run_groups(more, use_ref, q_ref, acc_ref, kv_refs, keys, wide, put)


def stage(use, q, acc, arrays, fresh, more, idle, units):
    rows = max(rows_of(case) for _, case, _ in fresh + more)
    used = sorted({i for _, case, _ in fresh + more for i, _, _ in case})
    fresh, more = (
        [
            (flag, [(used.index(i), start, stop) for i, start, stop in case], unroll)
            for flag, case, unroll in groups
        ]
        for groups in (fresh, more)
    )
    return pl.pallas_call(
        functools.partial(stage_kernel, fresh, more, idle),
        out_shape=(jax.ShapeDtypeStruct(acc.shape, F32), TOKEN),
        in_specs=[SMEM] + [VMEM] * (2 + len(used)),
        out_specs=(VMEM, VMEM),
        scratch_shapes=[pltpu.VMEM((rows, HD), BF16), pltpu.VMEM((rows, 2 * HD), BF16)],
        compiler_params=params(),
        cost_estimate=cost(units),
        name="add_blocks",
    )(use, q, *[arrays[i] for i in used], acc)


def online(q, keys, values, usable, running):
    top, total, mixed = running
    scores = lax.dot_general(q, keys, NT, preferred_element_type=F32) * SCALE
    if usable is not None:
        scores = jnp.where(usable, scores, -jnp.inf)
    fresh = jnp.maximum(top, jnp.max(scores, axis=1, keepdims=True))
    rescale = jnp.exp2(top - fresh)
    weights = jnp.exp2(scores - fresh)
    total = total * rescale + jnp.sum(weights, axis=1, keepdims=True)
    mixed = mixed * rescale + jnp.dot(weights.astype(BF16), values, preferred_element_type=F32)
    return fresh, total, mixed


def final_kernel(earlier, last, idle, use_ref, q_ref, *refs):
    kv_refs, (local_ref, acc_in, out_ref, keys, wide, worst) = refs[:-6], refs[-6:]
    worst[...] = jnp.zeros_like(worst)

    def put(r, across, weighted_sum):
        total = weighted_sum[:, HD:]
        worst[...] = jnp.maximum(
            worst[...], jnp.where((total > LOW) & (total < HIGH), 0.0, 1.0)
        )
        out_ref[:, across] = (weighted_sum[:, :HD] / total).astype(BF16)

    hand_over(use_ref, idle, acc_in, put)
    run_groups(last, use_ref, q_ref, acc_in, kv_refs, keys, wide, put)

    @pl.when(jnp.max(worst[...]) > 0.0)
    def _():
        tile = 128

        def redo(step, carry):
            r, t = step // (BLK // tile), step % (BLK // tile)
            here = pl.ds(pl.multiple_of(t * tile, tile), tile)
            across = pl.ds(pl.multiple_of(r * HD, HD), HD)
            q = q_ref[here, across]
            running = (
                jnp.full((tile, 1), -1e30, F32),
                jnp.zeros((tile, 1), F32),
                jnp.zeros((tile, HD), F32),
            )
            rows = t * tile + lax.broadcasted_iota(jnp.int32, (tile, BLK), 0)
            cols = lax.broadcasted_iota(jnp.int32, (tile, BLK), 1)
            running = online(q, local_ref[:, :HD], local_ref[:, HD:], cols <= rows, running)
            for flag, case, _ in earlier + last:

                def more(state, case=case):
                    for i, start, stop in case:
                        kv = kv_refs[i]
                        state = online(q, kv[start:stop, :HD], kv[start:stop, HD:], None, state)
                    return state

                running = lax.cond(use_ref[flag] != 0, more, lambda state: state, running)
            out_ref[here, across] = (running[2] / running[1]).astype(BF16)
            return carry

        lax.fori_loop(0, GROUP * (BLK // tile), redo, 0)


def final(use, q, acc, local_kv, arrays, earlier, last, idle):
    rows = max(rows_of(case) for _, case, _ in last)
    return pl.pallas_call(
        functools.partial(final_kernel, earlier, last, idle),
        out_shape=jax.ShapeDtypeStruct((BLK, GROUP * HD), BF16),
        in_specs=[SMEM] + [VMEM] * (3 + len(arrays)),
        out_specs=VMEM,
        scratch_shapes=[
            pltpu.VMEM((rows, HD), BF16),
            pltpu.VMEM((rows, 2 * HD), BF16),
            pltpu.VMEM((BLK, HD), F32),
        ],
        compiler_params=params(),
        cost_estimate=cost(4),
        name="last_blocks",
    )(use, q, *arrays, local_kv, acc)


SIBLING = [(s, s ^ 1) for s in range(16)]
PEER = [(s, s ^ 2) for s in range(16)]


def ahead(d, first=0):
    return [(s, s + 4 * d) for s in range(4 * first, 16 - 4 * d)]


def after(messages, token):
    def kernel(*refs):
        del refs

    return pl.pallas_call(
        kernel,
        out_shape=tuple(jax.ShapeDtypeStruct(x.shape, x.dtype) for x in messages),
        in_specs=[VMEM] * (len(messages) + 1),
        out_specs=(VMEM,) * len(messages),
        input_output_aliases={i: i for i in range(len(messages))},
        compiler_params=params(),
        name="hand_on",
    )(*messages, token)


def local(queries, key_states, value_states, passing_rows):
    me = lax.axis_index("seq")
    z, h, c = me // 4, (me // 2) % 2, me % 2
    move = functools.partial(lax.ppermute, axis_name="seq")

    def flags(*conditions):
        return jnp.stack([jnp.asarray(x).astype(jnp.int32) for x in conditions])

    kv_heads = key_states.shape[1] // HD
    rows = key_states.shape[0]
    both = jnp.concatenate(
        [key_states.reshape(rows, kv_heads, HD), value_states.reshape(rows, kv_heads, HD)], axis=2
    ).transpose(1, 0, 2)
    kv = lax.all_to_all(both, "head", split_axis=0, concat_axis=0, tiled=True).reshape(BLK, 2 * HD)

    anchor_side = move(kv[: 2 * HALF], perm=[(0, 1)])
    mine = select(flags(c), passing_rows, kv, anchor_side)
    peer = move(mine, perm=PEER)
    pair = join(flags(h), mine, peer)
    one = move(pair, perm=ahead(1))
    three = move(pair, perm=ahead(3))
    pair_side = move(pair, perm=SIBLING)

    def both(i):
        return ((i, 0, 2 * PASS), (i + 1, 0, 2 * PASS))

    def anchor(i):
        return ((i, 2 * PASS, 2 * PASS + HALF), (i + 1, 2 * PASS, 2 * PASS + HALF))

    arrays = [pair, pair_side] + [None] * 6
    near = (
        (0, ((0, PASS, 2 * PASS), (1, PASS, 2 * PASS)), GROUP),
        (1, ((1, 0, PASS),), GROUP),
        (2, anchor(0), 1),
    )
    fresh = ((3, both(2), GROUP),)
    more = ((4, anchor(2), 1), (5, both(4) + anchor(4), GROUP))
    last = ((6, both(6) + anchor(6), 2), (5, both(6), GROUP))
    use = flags(
        h == 1, c == 1, (z == 0) & (me > 0), z >= 1, z == 1, z == 3, z == 2, z == 0, z < 2
    )
    q = queries

    acc, token = first_part(use, q, kv, arrays[:2], near)
    (one,) = after((one,), token)
    (three,) = after((three,), token)
    two = move(one, perm=ahead(1, 1))
    arrays[2], arrays[3] = one, move(one, perm=SIBLING)
    arrays[4], arrays[5] = three, move(three, perm=SIBLING)
    acc, token = stage(use, q, acc, arrays, fresh, more, 7, 9)
    (two,) = after((two,), token)
    arrays[6], arrays[7] = two, move(two, perm=SIBLING)
    return final(use, q, acc, kv, arrays, near + fresh + more, last, 8)


def solution(mesh):
    in_specs = (
        P("seq", "head"),
        P(("seq", "head"), None),
        P(("seq", "head"), None),
        P("head", "seq"),
    )
    return jax.shard_map(
        local, mesh=mesh, in_specs=in_specs, out_specs=P("seq", "head"), check_vma=False
    )
```

```python
import functools

import jax
import jax.numpy as jnp
from jax import lax
from jax.experimental import pallas as pl
from jax.experimental.pallas import tpu as pltpu
from jax.sharding import PartitionSpec as P

HD = 128
GROUP = 8
BLK = 512
PASS = 256
HALF = 128
SIDE = 4
SCALE = float(HD**-0.5 * 1.4426950408889634)
LOW, HIGH = 2.0**-80, 2.0**100
BF16, F32 = jnp.bfloat16, jnp.float32
NT = (((1,), (1,)), ((), ()))
VMEM_BYTES = 24 * 2**20
SMEM = pl.BlockSpec(memory_space=pltpu.SMEM)
VMEM = pl.BlockSpec(memory_space=pltpu.VMEM)


TOKEN = jax.ShapeDtypeStruct((8, HD), F32)


def cost(units):
    return pl.CostEstimate(
        flops=int(units * 2 * 2 * GROUP * BLK * 256 * 256),
        bytes_accessed=1 << 20,
        transcendentals=int(units * GROUP * BLK * 256),
    )


def params():
    return pltpu.CompilerParams(vmem_limit_bytes=VMEM_BYTES)


def columns(r):
    return slice(r * HD, (r + 1) * HD)


def select_kernel(core_ref, rows_ref, kv_ref, side_ref, out_ref, half_ref):
    rows = rows_ref[...]
    ids = lax.broadcasted_iota(jnp.int32, (BLK, PASS), 0)
    picked = jnp.where(ids == rows, 1.0, 0.0).astype(BF16)
    out_ref[...] = lax.dot_general(
        picked, kv_ref[...], (((0,), (0,)), ((), ())), preferred_element_type=F32
    ).astype(BF16)

    @pl.when(core_ref[0] == 0)
    def _():
        half_ref[...] = kv_ref[:HALF]

    @pl.when(core_ref[0] != 0)
    def _():
        half_ref[...] = side_ref[HALF : 2 * HALF]


def select(core, rows, kv, side):
    return pl.pallas_call(
        select_kernel,
        out_shape=(
            jax.ShapeDtypeStruct((PASS, 2 * HD), BF16),
            jax.ShapeDtypeStruct((HALF, 2 * HD), BF16),
        ),
        in_specs=[SMEM, VMEM, VMEM, VMEM],
        out_specs=(VMEM, VMEM),
        compiler_params=params(),
        name="select_rows",
    )(core, rows, kv, side)


def join_kernel(where_ref, mine_ref, peer_ref, half_ref, peer_half_ref, out_ref):
    out_ref[:PASS] = mine_ref[...]
    out_ref[PASS : 2 * PASS] = peer_ref[...]

    @pl.when(where_ref[0] == 0)
    def _():
        out_ref[2 * PASS :] = half_ref[...]

    @pl.when(where_ref[0] != 0)
    def _():
        out_ref[2 * PASS :] = peer_half_ref[...]


def join(where, mine, peer, half, peer_half):
    return pl.pallas_call(
        join_kernel,
        out_shape=jax.ShapeDtypeStruct((2 * PASS + HALF, 2 * HD), BF16),
        in_specs=[SMEM, VMEM, VMEM, VMEM, VMEM],
        out_specs=VMEM,
        compiler_params=params(),
        name="join_rows",
    )(where, mine, peer, half, peer_half)


def powers(scores):
    return jnp.exp2(scores * SCALE).astype(BF16)


def first_kernel(groups, use_ref, q_ref, kv_ref, *refs):
    near_refs, (acc_ref, token_ref, keys_near, wide) = refs[:-4], refs[-4:]
    token_ref[...] = jnp.zeros_like(token_ref)
    wide[:BLK, :HD] = kv_ref[:, HD:]
    wide[:BLK, HD:] = jnp.ones((BLK, HD), BF16)
    half = BLK // 2
    rows = lax.broadcasted_iota(jnp.int32, (half, half), 0)
    cols = lax.broadcasted_iota(jnp.int32, (half, half), 1)
    causal = cols <= rows
    keys = kv_ref[:, :HD]

    for r in range(GROUP):
        q = q_ref[:, columns(r)]
        scores = lax.dot_general(q, keys[:half], NT, preferred_element_type=F32)
        first = powers(jnp.where(causal, scores[:half], -jnp.inf))
        second = powers(scores[half:])
        scores = lax.dot_general(q[half:], keys[half:], NT, preferred_element_type=F32)
        third = powers(jnp.where(causal, scores, -jnp.inf))
        acc_ref[r, :half] = jnp.dot(first, wide[:half], preferred_element_type=F32)
        acc_ref[r, half:] = jnp.dot(
            jnp.concatenate([second, third], axis=1), wide[:BLK], preferred_element_type=F32
        )

    def put(r, across, total):
        acc_ref[r] = total

    run_groups(groups, use_ref, q_ref, acc_ref, near_refs, keys_near, wide, put)


def first_part(use, q, kv, arrays, groups):
    rows = max(BLK, *[rows_of(case) for _, case, _ in groups])
    return pl.pallas_call(
        functools.partial(first_kernel, groups),
        out_shape=(jax.ShapeDtypeStruct((GROUP, BLK, 2 * HD), F32), TOKEN),
        in_specs=[SMEM] + [VMEM] * (2 + len(arrays)),
        out_specs=(VMEM, VMEM),
        scratch_shapes=[pltpu.VMEM((rows, HD), BF16), pltpu.VMEM((rows, 2 * HD), BF16)],
        compiler_params=params(),
        cost_estimate=cost(2.5),
        name="first_blocks",
    )(use, q, kv, *arrays)


def rows_of(case):
    return sum(stop - start for _, start, stop in case)


def heads(body, unroll):
    if unroll == GROUP:
        for r in range(GROUP):
            body(r, columns(r))
        return

    def step(r, carry):
        body(r, pl.ds(pl.multiple_of(r * HD, HD), HD))
        return carry

    lax.fori_loop(0, GROUP, step, 0, unroll=unroll)


def weighted(case, unroll, q_ref, acc_ref, kv_refs, keys, wide, put):
    at = 0
    for i, start, stop in case:
        end = at + stop - start
        keys[at:end] = kv_refs[i][start:stop, :HD]
        wide[at:end, :HD] = kv_refs[i][start:stop, HD:]
        wide[at:end, HD:] = jnp.ones((end - at, HD), BF16)
        at = end

    def body(r, across):
        scores = lax.dot_general(q_ref[:, across], keys[:at], NT, preferred_element_type=F32)
        put(r, across, acc_ref[r] + jnp.dot(powers(scores), wide[:at], preferred_element_type=F32))

    heads(body, unroll)


def run_groups(groups, use_ref, q_ref, acc_ref, kv_refs, keys, wide, put):
    for flag, case, unroll in groups:

        @pl.when(use_ref[flag] != 0)
        def _():
            weighted(case, unroll, q_ref, acc_ref, kv_refs, keys, wide, put)


def hand_over(use_ref, flag, acc_ref, put):
    @pl.when(use_ref[flag] != 0)
    def _():
        heads(lambda r, across: put(r, across, acc_ref[r]), 1)


def stage_kernel(fresh, more, idle, use_ref, q_ref, *refs):
    kv_refs, (acc_in, acc_ref, token_ref, keys, wide) = refs[:-5], refs[-5:]
    token_ref[...] = jnp.zeros_like(token_ref)

    def put(r, across, total):
        acc_ref[r] = total

    hand_over(use_ref, idle, acc_in, put)
    run_groups(fresh, use_ref, q_ref, acc_in, kv_refs, keys, wide, put)
    run_groups(more, use_ref, q_ref, acc_ref, kv_refs, keys, wide, put)


def stage(use, q, acc, arrays, fresh, more, idle, units):
    rows = max(rows_of(case) for _, case, _ in fresh + more)
    used = sorted({i for _, case, _ in fresh + more for i, _, _ in case})
    fresh, more = (
        [
            (flag, [(used.index(i), start, stop) for i, start, stop in case], unroll)
            for flag, case, unroll in groups
        ]
        for groups in (fresh, more)
    )
    return pl.pallas_call(
        functools.partial(stage_kernel, fresh, more, idle),
        out_shape=(jax.ShapeDtypeStruct(acc.shape, F32), TOKEN),
        in_specs=[SMEM] + [VMEM] * (2 + len(used)),
        out_specs=(VMEM, VMEM),
        scratch_shapes=[pltpu.VMEM((rows, HD), BF16), pltpu.VMEM((rows, 2 * HD), BF16)],
        compiler_params=params(),
        cost_estimate=cost(units),
        name="add_blocks",
    )(use, q, *[arrays[i] for i in used], acc)


def online(q, keys, values, usable, running):
    top, total, mixed = running
    scores = lax.dot_general(q, keys, NT, preferred_element_type=F32) * SCALE
    if usable is not None:
        scores = jnp.where(usable, scores, -jnp.inf)
    fresh = jnp.maximum(top, jnp.max(scores, axis=1, keepdims=True))
    rescale = jnp.exp2(top - fresh)
    weights = jnp.exp2(scores - fresh)
    total = total * rescale + jnp.sum(weights, axis=1, keepdims=True)
    mixed = mixed * rescale + jnp.dot(weights.astype(BF16), values, preferred_element_type=F32)
    return fresh, total, mixed


def final_kernel(earlier, last, idle, use_ref, q_ref, *refs):
    kv_refs, (local_ref, acc_in, result_ref, keys, wide, worst, out_ref, sems) = refs[:-8], refs[-8:]
    worst[...] = jnp.zeros_like(worst)

    def send(r, across):
        return pltpu.make_async_copy(
            out_ref.at[:, across], result_ref.at[:, across], sems.at[r]
        )

    def put(r, across, weighted_sum):
        total = weighted_sum[:, HD:]
        worst[...] = jnp.maximum(
            worst[...], jnp.where((total > LOW) & (total < HIGH), 0.0, 1.0)
        )
        out_ref[:, across] = (weighted_sum[:, :HD] / total).astype(BF16)
        send(r, across).start()

    hand_over(use_ref, idle, acc_in, put)
    run_groups(last, use_ref, q_ref, acc_in, kv_refs, keys, wide, put)

    for r in range(GROUP):
        send(r, columns(r)).wait()

    @pl.when(jnp.max(worst[...]) > 0.0)
    def _():
        tile = 128

        def redo(step, carry):
            r, t = step // (BLK // tile), step % (BLK // tile)
            here = pl.ds(pl.multiple_of(t * tile, tile), tile)
            across = pl.ds(pl.multiple_of(r * HD, HD), HD)
            q = q_ref[here, across]
            running = (
                jnp.full((tile, 1), -1e30, F32),
                jnp.zeros((tile, 1), F32),
                jnp.zeros((tile, HD), F32),
            )
            rows = t * tile + lax.broadcasted_iota(jnp.int32, (tile, BLK), 0)
            cols = lax.broadcasted_iota(jnp.int32, (tile, BLK), 1)
            running = online(q, local_ref[:, :HD], local_ref[:, HD:], cols <= rows, running)
            for flag, case, _ in earlier + last:

                def more(state, case=case):
                    for i, start, stop in case:
                        kv = kv_refs[i]
                        state = online(q, kv[start:stop, :HD], kv[start:stop, HD:], None, state)
                    return state

                running = lax.cond(use_ref[flag] != 0, more, lambda state: state, running)
            out_ref[here, across] = (running[2] / running[1]).astype(BF16)
            return carry

        lax.fori_loop(0, GROUP * (BLK // tile), redo, 0)
        pltpu.sync_copy(out_ref, result_ref)


def final(use, q, acc, local_kv, arrays, earlier, last, idle):
    rows = max(rows_of(case) for _, case, _ in last)
    return pl.pallas_call(
        functools.partial(final_kernel, earlier, last, idle),
        out_shape=jax.ShapeDtypeStruct((BLK, GROUP * HD), BF16),
        in_specs=[SMEM] + [VMEM] * (3 + len(arrays)),
        out_specs=pl.BlockSpec(memory_space=pl.ANY),
        scratch_shapes=[
            pltpu.VMEM((rows, HD), BF16),
            pltpu.VMEM((rows, 2 * HD), BF16),
            pltpu.VMEM((BLK, HD), F32),
            pltpu.VMEM((BLK, GROUP * HD), BF16),
            pltpu.SemaphoreType.DMA((GROUP,)),
        ],
        compiler_params=params(),
        cost_estimate=cost(4),
        name="last_blocks",
    )(use, q, *arrays, local_kv, acc)


SIBLING = [(s, s ^ 1) for s in range(16)]
PEER = [(s, s ^ 2) for s in range(16)]


def ahead(d, first=0):
    return [(s, s + 4 * d) for s in range(4 * first, 16 - 4 * d)]


def after(messages, token):
    def kernel(*refs):
        del refs

    return pl.pallas_call(
        kernel,
        out_shape=tuple(jax.ShapeDtypeStruct(x.shape, x.dtype) for x in messages),
        in_specs=[VMEM] * (len(messages) + 1),
        out_specs=(VMEM,) * len(messages),
        input_output_aliases={i: i for i in range(len(messages))},
        compiler_params=params(),
        name="hand_on",
    )(*messages, token)


def local(queries, key_states, value_states, passing_rows):
    me = lax.axis_index("seq")
    z, h, c = me // 4, (me // 2) % 2, me % 2
    move = functools.partial(lax.ppermute, axis_name="seq")

    def flags(*conditions):
        return jnp.stack([jnp.asarray(x).astype(jnp.int32) for x in conditions])

    kv_heads = key_states.shape[1] // HD
    rows = key_states.shape[0]
    both = jnp.concatenate(
        [key_states.reshape(rows, kv_heads, HD), value_states.reshape(rows, kv_heads, HD)], axis=2
    ).transpose(1, 0, 2)
    kv = lax.all_to_all(both, "head", split_axis=0, concat_axis=0, tiled=True).reshape(BLK, 2 * HD)

    anchor_side = move(kv[: 2 * HALF], perm=[(0, 1)])
    mine, half = select(flags(c), passing_rows, kv, anchor_side)
    peer = move(mine, perm=PEER)
    peer_half = move(half, perm=[(0, 2), (1, 3)])
    pair = join(flags(h), mine, peer, half, peer_half)
    one = move(pair, perm=ahead(1))
    three = move(pair, perm=ahead(3))

    def both(i):
        return ((i, 0, 2 * PASS), (i + 1, 0, 2 * PASS))

    def anchor(i):
        return ((i, 2 * PASS, 2 * PASS + HALF), (i + 1, 2 * PASS, 2 * PASS + HALF))

    arrays = [pair] + [None] * 7
    near = ((0, ((0, PASS, 2 * PASS),), GROUP),)
    fresh = ((1, both(2), GROUP),)
    more = ((2, anchor(2), 1), (3, both(4) + anchor(4), GROUP))
    side = (
        (4, ((1, 0, 2 * PASS),), GROUP),
        (5, ((1, 0, PASS),), SIDE),
        (6, ((1, PASS, 2 * PASS),), SIDE),
    )
    side_more = ((7, anchor(0), 1),)
    last = ((8, both(6) + anchor(6), 4), (3, both(6), GROUP))
    use = flags(
        h == 1, z >= 1, z == 1, z == 3,
        (h == 1) & (c == 1), (h == 0) & (c == 1), (h == 1) & (c == 0),
        (z == 0) & (me > 0), z == 2, z == 0, h + c == 0, z < 2,
    )
    q = queries

    acc, token = first_part(use, q, kv, arrays[:1], near)
    (one,) = after((one,), token)
    (three,) = after((three,), token)
    arrays[1] = move(after((pair,), token)[0], perm=SIBLING)
    two = move(one, perm=ahead(1, 1))
    arrays[2], arrays[3] = one, move(one, perm=SIBLING)
    arrays[4], arrays[5] = three, move(three, perm=SIBLING)
    acc, token = stage(use, q, acc, arrays, fresh, more, 9, 9)
    (two,) = after((two,), token)
    arrays[6], arrays[7] = two, move(two, perm=SIBLING)
    acc, _ = stage(use, q, acc, arrays, side, side_more, 10, 2)
    return final(use, q, acc, kv, arrays, near + fresh + more + side + side_more, last, 11)


def solution(mesh):
    in_specs = (
        P("seq", "head"),
        P(("seq", "head"), None),
        P(("seq", "head"), None),
        P("head", "seq"),
    )
    return jax.shard_map(
        local, mesh=mesh, in_specs=in_specs, out_specs=P("seq", "head"), check_vma=False
    )
```

```python
import functools

import jax
import jax.numpy as jnp
from jax import lax
from jax.experimental import pallas as pl
from jax.experimental.pallas import tpu as pltpu
from jax.sharding import PartitionSpec as P

HD = 128
GROUP = 8
BLK = 512
PASS = 256
HALF = 128
SIDE = 4
SCALE = float(HD**-0.5 * 1.4426950408889634)
LOW, HIGH = 2.0**-80, 2.0**100
BF16, F32 = jnp.bfloat16, jnp.float32
NT = (((1,), (1,)), ((), ()))
VMEM_BYTES = 24 * 2**20
SMEM = pl.BlockSpec(memory_space=pltpu.SMEM)
VMEM = pl.BlockSpec(memory_space=pltpu.VMEM)


TOKEN = jax.ShapeDtypeStruct((8, HD), F32)


def cost(units):
    return pl.CostEstimate(
        flops=int(units * 2 * 2 * GROUP * BLK * 256 * 256),
        bytes_accessed=1 << 20,
        transcendentals=int(units * GROUP * BLK * 256),
    )


def params():
    return pltpu.CompilerParams(vmem_limit_bytes=VMEM_BYTES)


def columns(r):
    return slice(r * HD, (r + 1) * HD)


def select_kernel(rows_ref, kv_ref, out_ref):
    ids = lax.broadcasted_iota(jnp.int32, (BLK, PASS), 0)
    picked = jnp.where(ids == rows_ref[...], 1.0, 0.0).astype(BF16)
    out_ref[...] = lax.dot_general(
        picked, kv_ref[...], (((0,), (0,)), ((), ())), preferred_element_type=F32
    ).astype(BF16)


def select(rows, kv):
    return pl.pallas_call(
        select_kernel,
        out_shape=jax.ShapeDtypeStruct((PASS, 2 * HD), BF16),
        in_specs=[VMEM, VMEM],
        out_specs=VMEM,
        compiler_params=params(),
        name="select_rows",
    )(rows, kv)


def join_kernel(me_ref, mine_ref, peer_ref, kv_ref, *refs):
    halves, out_ref = refs[:-1], refs[-1]
    out_ref[:PASS] = mine_ref[...]
    out_ref[PASS : 2 * PASS] = peer_ref[...]
    out_ref[2 * PASS :] = kv_ref[:HALF]
    for block, half_ref in enumerate(halves):

        @pl.when(me_ref[0] == block + 1)
        def _():
            out_ref[2 * PASS :] = half_ref[...]


def join(me, mine, peer, kv, halves):
    return pl.pallas_call(
        join_kernel,
        out_shape=jax.ShapeDtypeStruct((2 * PASS + HALF, 2 * HD), BF16),
        in_specs=[SMEM] + [VMEM] * (3 + len(halves)),
        out_specs=VMEM,
        compiler_params=params(),
        name="join_rows",
    )(me, mine, peer, kv, *halves)


def powers(scores):
    return jnp.exp2(scores * SCALE).astype(BF16)


def first_kernel(groups, use_ref, q_ref, kv_ref, *refs):
    near_refs, (acc_ref, token_ref, keys_near, wide) = refs[:-4], refs[-4:]
    token_ref[...] = jnp.zeros_like(token_ref)
    wide[:BLK, :HD] = kv_ref[:, HD:]
    wide[:BLK, HD:] = jnp.ones((BLK, HD), BF16)
    half = BLK // 2
    rows = lax.broadcasted_iota(jnp.int32, (half, half), 0)
    cols = lax.broadcasted_iota(jnp.int32, (half, half), 1)
    causal = cols <= rows
    keys = kv_ref[:, :HD]

    for r in range(GROUP):
        q = q_ref[:, columns(r)]
        scores = lax.dot_general(q, keys[:half], NT, preferred_element_type=F32)
        first = powers(jnp.where(causal, scores[:half], -jnp.inf))
        second = powers(scores[half:])
        scores = lax.dot_general(q[half:], keys[half:], NT, preferred_element_type=F32)
        third = powers(jnp.where(causal, scores, -jnp.inf))
        acc_ref[r, :half] = jnp.dot(first, wide[:half], preferred_element_type=F32)
        acc_ref[r, half:] = jnp.dot(
            jnp.concatenate([second, third], axis=1), wide[:BLK], preferred_element_type=F32
        )

    def put(r, across, total):
        acc_ref[r] = total

    run_groups(groups, use_ref, q_ref, acc_ref, near_refs, keys_near, wide, put)


def first_part(use, q, kv, arrays, groups):
    rows = max(BLK, *[rows_of(case) for _, case, _ in groups])
    return pl.pallas_call(
        functools.partial(first_kernel, groups),
        out_shape=(jax.ShapeDtypeStruct((GROUP, BLK, 2 * HD), F32), TOKEN),
        in_specs=[SMEM] + [VMEM] * (2 + len(arrays)),
        out_specs=(VMEM, VMEM),
        scratch_shapes=[pltpu.VMEM((rows, HD), BF16), pltpu.VMEM((rows, 2 * HD), BF16)],
        compiler_params=params(),
        cost_estimate=cost(2.5),
        name="first_blocks",
    )(use, q, kv, *arrays)


def rows_of(case):
    return sum(stop - start for _, start, stop in case)


def heads(body, unroll):
    if unroll == GROUP:
        for r in range(GROUP):
            body(r, columns(r))
        return

    def step(r, carry):
        body(r, pl.ds(pl.multiple_of(r * HD, HD), HD))
        return carry

    lax.fori_loop(0, GROUP, step, 0, unroll=unroll)


def weighted(case, unroll, q_ref, acc_ref, kv_refs, keys, wide, put):
    at = 0
    for i, start, stop in case:
        end = at + stop - start
        keys[at:end] = kv_refs[i][start:stop, :HD]
        wide[at:end, :HD] = kv_refs[i][start:stop, HD:]
        wide[at:end, HD:] = jnp.ones((end - at, HD), BF16)
        at = end

    def body(r, across):
        scores = lax.dot_general(q_ref[:, across], keys[:at], NT, preferred_element_type=F32)
        put(r, across, acc_ref[r] + jnp.dot(powers(scores), wide[:at], preferred_element_type=F32))

    heads(body, unroll)


def run_groups(groups, use_ref, q_ref, acc_ref, kv_refs, keys, wide, put):
    for flag, case, unroll in groups:

        @pl.when(use_ref[flag] != 0)
        def _():
            weighted(case, unroll, q_ref, acc_ref, kv_refs, keys, wide, put)


def hand_over(use_ref, flag, acc_ref, put):
    @pl.when(use_ref[flag] != 0)
    def _():
        heads(lambda r, across: put(r, across, acc_ref[r]), 1)


def stage_kernel(fresh, more, idle, use_ref, q_ref, *refs):
    kv_refs, (acc_in, acc_ref, token_ref, keys, wide) = refs[:-5], refs[-5:]
    token_ref[...] = jnp.zeros_like(token_ref)

    def put(r, across, total):
        acc_ref[r] = total

    hand_over(use_ref, idle, acc_in, put)
    run_groups(fresh, use_ref, q_ref, acc_in, kv_refs, keys, wide, put)
    run_groups(more, use_ref, q_ref, acc_ref, kv_refs, keys, wide, put)


def stage(use, q, acc, arrays, fresh, more, idle, units):
    rows = max(rows_of(case) for _, case, _ in fresh + more)
    used = sorted({i for _, case, _ in fresh + more for i, _, _ in case})
    fresh, more = (
        [
            (flag, [(used.index(i), start, stop) for i, start, stop in case], unroll)
            for flag, case, unroll in groups
        ]
        for groups in (fresh, more)
    )
    return pl.pallas_call(
        functools.partial(stage_kernel, fresh, more, idle),
        out_shape=(jax.ShapeDtypeStruct(acc.shape, F32), TOKEN),
        in_specs=[SMEM] + [VMEM] * (2 + len(used)),
        out_specs=(VMEM, VMEM),
        scratch_shapes=[pltpu.VMEM((rows, HD), BF16), pltpu.VMEM((rows, 2 * HD), BF16)],
        compiler_params=params(),
        cost_estimate=cost(units),
        name="add_blocks",
    )(use, q, *[arrays[i] for i in used], acc)


def online(q, keys, values, usable, running):
    top, total, mixed = running
    scores = lax.dot_general(q, keys, NT, preferred_element_type=F32) * SCALE
    if usable is not None:
        scores = jnp.where(usable, scores, -jnp.inf)
    fresh = jnp.maximum(top, jnp.max(scores, axis=1, keepdims=True))
    rescale = jnp.exp2(top - fresh)
    weights = jnp.exp2(scores - fresh)
    total = total * rescale + jnp.sum(weights, axis=1, keepdims=True)
    mixed = mixed * rescale + jnp.dot(weights.astype(BF16), values, preferred_element_type=F32)
    return fresh, total, mixed


def final_kernel(earlier, last, idle, use_ref, q_ref, *refs):
    kv_refs, (local_ref, acc_in, result_ref, keys, wide, worst, out_ref, sems) = refs[:-8], refs[-8:]
    worst[...] = jnp.zeros_like(worst)

    def send(r, across):
        return pltpu.make_async_copy(
            out_ref.at[:, across], result_ref.at[:, across], sems.at[r]
        )

    def put(r, across, weighted_sum):
        total = weighted_sum[:, HD:]
        worst[...] = jnp.maximum(
            worst[...], jnp.where((total > LOW) & (total < HIGH), 0.0, 1.0)
        )
        out_ref[:, across] = (weighted_sum[:, :HD] / total).astype(BF16)
        send(r, across).start()

    hand_over(use_ref, idle, acc_in, put)
    run_groups(last, use_ref, q_ref, acc_in, kv_refs, keys, wide, put)

    for r in range(GROUP):
        send(r, columns(r)).wait()

    @pl.when(jnp.max(worst[...]) > 0.0)
    def _():
        tile = 128

        def redo(step, carry):
            r, t = step // (BLK // tile), step % (BLK // tile)
            here = pl.ds(pl.multiple_of(t * tile, tile), tile)
            across = pl.ds(pl.multiple_of(r * HD, HD), HD)
            q = q_ref[here, across]
            running = (
                jnp.full((tile, 1), -1e30, F32),
                jnp.zeros((tile, 1), F32),
                jnp.zeros((tile, HD), F32),
            )
            rows = t * tile + lax.broadcasted_iota(jnp.int32, (tile, BLK), 0)
            cols = lax.broadcasted_iota(jnp.int32, (tile, BLK), 1)
            running = online(q, local_ref[:, :HD], local_ref[:, HD:], cols <= rows, running)
            for flag, case, _ in earlier + last:

                def more(state, case=case):
                    for i, start, stop in case:
                        kv = kv_refs[i]
                        state = online(q, kv[start:stop, :HD], kv[start:stop, HD:], None, state)
                    return state

                running = lax.cond(use_ref[flag] != 0, more, lambda state: state, running)
            out_ref[here, across] = (running[2] / running[1]).astype(BF16)
            return carry

        lax.fori_loop(0, GROUP * (BLK // tile), redo, 0)
        pltpu.sync_copy(out_ref, result_ref)


def final(use, q, acc, local_kv, arrays, earlier, last, idle):
    rows = max(rows_of(case) for _, case, _ in last)
    return pl.pallas_call(
        functools.partial(final_kernel, earlier, last, idle),
        out_shape=jax.ShapeDtypeStruct((BLK, GROUP * HD), BF16),
        in_specs=[SMEM] + [VMEM] * (3 + len(arrays)),
        out_specs=pl.BlockSpec(memory_space=pl.ANY),
        scratch_shapes=[
            pltpu.VMEM((rows, HD), BF16),
            pltpu.VMEM((rows, 2 * HD), BF16),
            pltpu.VMEM((BLK, HD), F32),
            pltpu.VMEM((BLK, GROUP * HD), BF16),
            pltpu.SemaphoreType.DMA((GROUP,)),
        ],
        compiler_params=params(),
        cost_estimate=cost(4),
        name="last_blocks",
    )(use, q, *arrays, local_kv, acc)


SIBLING = [(s, s ^ 1) for s in range(16)]
PEER = [(s, s ^ 2) for s in range(16)]


def ahead(d, first=0):
    return [(s, s + 4 * d) for s in range(4 * first, 16 - 4 * d)]


def after(messages, token):
    def kernel(*refs):
        del refs

    return pl.pallas_call(
        kernel,
        out_shape=tuple(jax.ShapeDtypeStruct(x.shape, x.dtype) for x in messages),
        in_specs=[VMEM] * (len(messages) + 1),
        out_specs=(VMEM,) * len(messages),
        input_output_aliases={i: i for i in range(len(messages))},
        compiler_params=params(),
        name="hand_on",
    )(*messages, token)


def local(queries, key_states, value_states, passing_rows):
    me = lax.axis_index("seq")
    z, h, c = me // 4, (me // 2) % 2, me % 2
    move = functools.partial(lax.ppermute, axis_name="seq")

    def flags(*conditions):
        return jnp.stack([jnp.asarray(x).astype(jnp.int32) for x in conditions])

    kv_heads = key_states.shape[1] // HD
    rows = key_states.shape[0]
    both = jnp.concatenate(
        [key_states.reshape(rows, kv_heads, HD), value_states.reshape(rows, kv_heads, HD)], axis=2
    ).transpose(1, 0, 2)
    kv = lax.all_to_all(both, "head", split_axis=0, concat_axis=0, tiled=True).reshape(BLK, 2 * HD)

    mine = select(passing_rows, kv)
    peer = move(mine, perm=PEER)
    low, high = kv[:HALF], kv[HALF : 2 * HALF]
    halves = [
        move(half, perm=[(0, block)]) for block, half in ((1, high), (2, low), (3, high))
    ]
    pair = join(flags(me), mine, peer, kv, halves)
    one = move(pair, perm=ahead(1))
    three = move(pair, perm=ahead(3))

    def both(i):
        return ((i, 0, 2 * PASS), (i + 1, 0, 2 * PASS))

    def anchor(i):
        return ((i, 2 * PASS, 2 * PASS + HALF), (i + 1, 2 * PASS, 2 * PASS + HALF))

    arrays = [pair] + [None] * 7
    near = ((0, ((0, PASS, 2 * PASS),), GROUP),)
    fresh = ((1, both(2), GROUP),)
    more = ((2, anchor(2), 1), (3, both(4) + anchor(4), GROUP))
    side = (
        (4, ((1, 0, 2 * PASS),), GROUP),
        (5, ((1, 0, PASS),), SIDE),
        (6, ((1, PASS, 2 * PASS),), SIDE),
    )
    side_more = ((7, anchor(0), 1),)
    last = ((8, both(6) + anchor(6), 4), (3, both(6), GROUP))
    use = flags(
        h == 1, z >= 1, z == 1, z == 3,
        (h == 1) & (c == 1), (h == 0) & (c == 1), (h == 1) & (c == 0),
        (z == 0) & (me > 0), z == 2, z == 0, h + c == 0, z < 2,
    )
    q = queries

    acc, token = first_part(use, q, kv, arrays[:1], near)
    (one,) = after((one,), token)
    (three,) = after((three,), token)
    arrays[1] = move(after((pair,), token)[0], perm=SIBLING)
    two = move(one, perm=ahead(1, 1))
    arrays[2], arrays[3] = one, move(one, perm=SIBLING)
    arrays[4], arrays[5] = three, move(three, perm=SIBLING)
    acc, token = stage(use, q, acc, arrays, fresh, more, 9, 9)
    (two,) = after((two,), token)
    arrays[6], arrays[7] = two, move(two, perm=SIBLING)
    acc, _ = stage(use, q, acc, arrays, side, side_more, 10, 2)
    return final(use, q, acc, kv, arrays, near + fresh + more + side + side_more, last, 11)


def solution(mesh):
    in_specs = (
        P("seq", "head"),
        P(("seq", "head"), None),
        P(("seq", "head"), None),
        P("head", "seq"),
    )
    return jax.shard_map(
        local, mesh=mesh, in_specs=in_specs, out_specs=P("seq", "head"), check_vma=False
    )
```

```python
import functools

import jax
import jax.numpy as jnp
from jax import lax
from jax.experimental import pallas as pl
from jax.experimental.pallas import tpu as pltpu
from jax.sharding import PartitionSpec as P

HD = 128
GROUP = 8
BLK = 512
PASS = 256
HALF = 128
SIDE = 8
SCALE = float(HD**-0.5 * 1.4426950408889634)
LOW, HIGH = 2.0**-80, 2.0**100
BF16, F32 = jnp.bfloat16, jnp.float32
NT = (((1,), (1,)), ((), ()))
VMEM_BYTES = 24 * 2**20
SMEM = pl.BlockSpec(memory_space=pltpu.SMEM)
VMEM = pl.BlockSpec(memory_space=pltpu.VMEM)


TOKEN = jax.ShapeDtypeStruct((8, HD), F32)


def cost(units):
    return pl.CostEstimate(
        flops=int(units * 2 * 2 * GROUP * BLK * 256 * 256),
        bytes_accessed=1 << 20,
        transcendentals=int(units * GROUP * BLK * 256),
    )


def params():
    return pltpu.CompilerParams(vmem_limit_bytes=VMEM_BYTES)


def columns(r):
    return slice(r * HD, (r + 1) * HD)


def mark_kernel(rows_ref, picked_ref):
    ids = lax.broadcasted_iota(jnp.int32, (BLK, PASS), 0)
    picked_ref[...] = jnp.where(ids == rows_ref[...], 1.0, 0.0).astype(BF16)


def mark(rows):
    return pl.pallas_call(
        mark_kernel,
        out_shape=jax.ShapeDtypeStruct((BLK, PASS), BF16),
        in_specs=[VMEM],
        out_specs=VMEM,
        compiler_params=params(),
        cost_estimate=cost(1),
        name="mark_rows",
    )(rows)


def select_kernel(picked_ref, parts_ref, out_ref, kv_ref):
    count = parts_ref.shape[2]
    for part in range(GROUP):
        rows = slice(part * count, (part + 1) * count)
        kv_ref[rows, :HD] = parts_ref[part, 0]
        kv_ref[rows, HD:] = parts_ref[part, 1]
    out_ref[...] = lax.dot_general(
        picked_ref[...], kv_ref[...], (((0,), (0,)), ((), ())), preferred_element_type=F32
    ).astype(BF16)


def select(picked, parts):
    return pl.pallas_call(
        select_kernel,
        out_shape=(
            jax.ShapeDtypeStruct((PASS, 2 * HD), BF16),
            jax.ShapeDtypeStruct((BLK, 2 * HD), BF16),
        ),
        in_specs=[VMEM, VMEM],
        out_specs=(VMEM, VMEM),
        compiler_params=params(),
        name="select_rows",
    )(picked, parts)


def join_kernel(me_ref, mine_ref, peer_ref, kv_ref, *refs):
    halves, out_ref = refs[:-1], refs[-1]
    out_ref[:PASS] = mine_ref[...]
    out_ref[PASS : 2 * PASS] = peer_ref[...]
    out_ref[2 * PASS :] = kv_ref[:HALF]
    for block, half_ref in enumerate(halves):

        @pl.when(me_ref[0] == block + 1)
        def _():
            out_ref[2 * PASS :] = half_ref[...]


def join(me, mine, peer, kv, halves):
    return pl.pallas_call(
        join_kernel,
        out_shape=jax.ShapeDtypeStruct((2 * PASS + HALF, 2 * HD), BF16),
        in_specs=[SMEM] + [VMEM] * (3 + len(halves)),
        out_specs=VMEM,
        compiler_params=params(),
        name="join_rows",
    )(me, mine, peer, kv, *halves)


def powers(scores):
    return jnp.exp2(scores * SCALE).astype(BF16)


def first_kernel(groups, use_ref, q_ref, kv_ref, *refs):
    near_refs, (acc_ref, token_ref, keys_near, wide) = refs[:-4], refs[-4:]
    token_ref[...] = jnp.zeros_like(token_ref)
    wide[:BLK, :HD] = kv_ref[:, HD:]
    wide[:BLK, HD:] = jnp.ones((BLK, HD), BF16)
    half = BLK // 2
    rows = lax.broadcasted_iota(jnp.int32, (half, half), 0)
    cols = lax.broadcasted_iota(jnp.int32, (half, half), 1)
    causal = cols <= rows
    keys = kv_ref[:, :HD]

    for r in range(GROUP):
        q = q_ref[:, columns(r)]
        scores = lax.dot_general(q, keys[:half], NT, preferred_element_type=F32)
        first = powers(jnp.where(causal, scores[:half], -jnp.inf))
        second = powers(scores[half:])
        scores = lax.dot_general(q[half:], keys[half:], NT, preferred_element_type=F32)
        third = powers(jnp.where(causal, scores, -jnp.inf))
        acc_ref[r, :half] = jnp.dot(first, wide[:half], preferred_element_type=F32)
        acc_ref[r, half:] = jnp.dot(
            jnp.concatenate([second, third], axis=1), wide[:BLK], preferred_element_type=F32
        )

    def put(r, across, total):
        acc_ref[r] = total

    run_groups(groups, use_ref, q_ref, acc_ref, near_refs, keys_near, wide, put)


def first_part(use, q, kv, arrays, groups):
    rows = max(BLK, *[rows_of(case) for _, case, _ in groups])
    return pl.pallas_call(
        functools.partial(first_kernel, groups),
        out_shape=(jax.ShapeDtypeStruct((GROUP, BLK, 2 * HD), F32), TOKEN),
        in_specs=[SMEM] + [VMEM] * (2 + len(arrays)),
        out_specs=(VMEM, VMEM),
        scratch_shapes=[pltpu.VMEM((rows, HD), BF16), pltpu.VMEM((rows, 2 * HD), BF16)],
        compiler_params=params(),
        cost_estimate=cost(2.5),
        name="first_blocks",
    )(use, q, kv, *arrays)


def rows_of(case):
    return sum(stop - start for _, start, stop in case)


def heads(body, unroll):
    if unroll == GROUP:
        for r in range(GROUP):
            body(r, columns(r))
        return

    def step(r, carry):
        body(r, pl.ds(pl.multiple_of(r * HD, HD), HD))
        return carry

    lax.fori_loop(0, GROUP, step, 0, unroll=unroll)


def weighted(case, unroll, q_ref, acc_ref, kv_refs, keys, wide, put):
    at = 0
    for i, start, stop in case:
        end = at + stop - start
        keys[at:end] = kv_refs[i][start:stop, :HD]
        wide[at:end, :HD] = kv_refs[i][start:stop, HD:]
        wide[at:end, HD:] = jnp.ones((end - at, HD), BF16)
        at = end

    def body(r, across):
        scores = lax.dot_general(q_ref[:, across], keys[:at], NT, preferred_element_type=F32)
        put(r, across, acc_ref[r] + jnp.dot(powers(scores), wide[:at], preferred_element_type=F32))

    heads(body, unroll)


def run_groups(groups, use_ref, q_ref, acc_ref, kv_refs, keys, wide, put):
    for flag, case, unroll in groups:

        @pl.when(use_ref[flag] != 0)
        def _():
            weighted(case, unroll, q_ref, acc_ref, kv_refs, keys, wide, put)


def hand_over(use_ref, flag, acc_ref, put):
    @pl.when(use_ref[flag] != 0)
    def _():
        heads(lambda r, across: put(r, across, acc_ref[r]), 1)


def stage_kernel(fresh, more, idle, use_ref, q_ref, *refs):
    kv_refs, (acc_in, acc_ref, token_ref, keys, wide) = refs[:-5], refs[-5:]
    token_ref[...] = jnp.zeros_like(token_ref)

    def put(r, across, total):
        acc_ref[r] = total

    hand_over(use_ref, idle, acc_in, put)
    run_groups(fresh, use_ref, q_ref, acc_in, kv_refs, keys, wide, put)
    run_groups(more, use_ref, q_ref, acc_ref, kv_refs, keys, wide, put)


def stage(use, q, acc, arrays, fresh, more, idle, units):
    rows = max(rows_of(case) for _, case, _ in fresh + more)
    used = sorted({i for _, case, _ in fresh + more for i, _, _ in case})
    fresh, more = (
        [
            (flag, [(used.index(i), start, stop) for i, start, stop in case], unroll)
            for flag, case, unroll in groups
        ]
        for groups in (fresh, more)
    )
    return pl.pallas_call(
        functools.partial(stage_kernel, fresh, more, idle),
        out_shape=(jax.ShapeDtypeStruct(acc.shape, F32), TOKEN),
        in_specs=[SMEM] + [VMEM] * (2 + len(used)),
        out_specs=(VMEM, VMEM),
        scratch_shapes=[pltpu.VMEM((rows, HD), BF16), pltpu.VMEM((rows, 2 * HD), BF16)],
        compiler_params=params(),
        cost_estimate=cost(units),
        name="add_blocks",
    )(use, q, *[arrays[i] for i in used], acc)


def online(q, keys, values, usable, running):
    top, total, mixed = running
    scores = lax.dot_general(q, keys, NT, preferred_element_type=F32) * SCALE
    if usable is not None:
        scores = jnp.where(usable, scores, -jnp.inf)
    fresh = jnp.maximum(top, jnp.max(scores, axis=1, keepdims=True))
    rescale = jnp.exp2(top - fresh)
    weights = jnp.exp2(scores - fresh)
    total = total * rescale + jnp.sum(weights, axis=1, keepdims=True)
    mixed = mixed * rescale + jnp.dot(weights.astype(BF16), values, preferred_element_type=F32)
    return fresh, total, mixed


def final_kernel(earlier, last, idle, use_ref, q_ref, *refs):
    kv_refs, (local_ref, acc_in, result_ref, keys, wide, worst, out_ref, sems) = refs[:-8], refs[-8:]
    worst[...] = jnp.zeros_like(worst)

    def send(r, across):
        return pltpu.make_async_copy(
            out_ref.at[:, across], result_ref.at[:, across], sems.at[r]
        )

    def put(r, across, weighted_sum):
        total = weighted_sum[:, HD:]
        worst[...] = jnp.maximum(
            worst[...], jnp.where((total > LOW) & (total < HIGH), 0.0, 1.0)
        )
        out_ref[:, across] = (weighted_sum[:, :HD] / total).astype(BF16)
        send(r, across).start()

    hand_over(use_ref, idle, acc_in, put)
    run_groups(last, use_ref, q_ref, acc_in, kv_refs, keys, wide, put)

    for r in range(GROUP):
        send(r, columns(r)).wait()

    @pl.when(jnp.max(worst[...]) > 0.0)
    def _():
        tile = 128

        def redo(step, carry):
            r, t = step // (BLK // tile), step % (BLK // tile)
            here = pl.ds(pl.multiple_of(t * tile, tile), tile)
            across = pl.ds(pl.multiple_of(r * HD, HD), HD)
            q = q_ref[here, across]
            running = (
                jnp.full((tile, 1), -1e30, F32),
                jnp.zeros((tile, 1), F32),
                jnp.zeros((tile, HD), F32),
            )
            rows = t * tile + lax.broadcasted_iota(jnp.int32, (tile, BLK), 0)
            cols = lax.broadcasted_iota(jnp.int32, (tile, BLK), 1)
            running = online(q, local_ref[:, :HD], local_ref[:, HD:], cols <= rows, running)
            for flag, case, _ in earlier + last:

                def more(state, case=case):
                    for i, start, stop in case:
                        kv = kv_refs[i]
                        state = online(q, kv[start:stop, :HD], kv[start:stop, HD:], None, state)
                    return state

                running = lax.cond(use_ref[flag] != 0, more, lambda state: state, running)
            out_ref[here, across] = (running[2] / running[1]).astype(BF16)
            return carry

        lax.fori_loop(0, GROUP * (BLK // tile), redo, 0)
        pltpu.sync_copy(out_ref, result_ref)


def final(use, q, acc, local_kv, arrays, earlier, last, idle):
    rows = max(rows_of(case) for _, case, _ in last)
    return pl.pallas_call(
        functools.partial(final_kernel, earlier, last, idle),
        out_shape=jax.ShapeDtypeStruct((BLK, GROUP * HD), BF16),
        in_specs=[SMEM] + [VMEM] * (3 + len(arrays)),
        out_specs=pl.BlockSpec(memory_space=pl.ANY),
        scratch_shapes=[
            pltpu.VMEM((rows, HD), BF16),
            pltpu.VMEM((rows, 2 * HD), BF16),
            pltpu.VMEM((BLK, HD), F32),
            pltpu.VMEM((BLK, GROUP * HD), BF16),
            pltpu.SemaphoreType.DMA((GROUP,)),
        ],
        compiler_params=params(),
        cost_estimate=cost(4),
        name="last_blocks",
    )(use, q, *arrays, local_kv, acc)


SIBLING = [(s, s ^ 1) for s in range(16)]
PEER = [(s, s ^ 2) for s in range(16)]


def ahead(d, first=0):
    return [(s, s + 4 * d) for s in range(4 * first, 16 - 4 * d)]


def after(messages, token):
    def kernel(*refs):
        del refs

    return pl.pallas_call(
        kernel,
        out_shape=tuple(jax.ShapeDtypeStruct(x.shape, x.dtype) for x in messages),
        in_specs=[VMEM] * (len(messages) + 1),
        out_specs=(VMEM,) * len(messages),
        input_output_aliases={i: i for i in range(len(messages))},
        compiler_params=params(),
        name="hand_on",
    )(*messages, token)


def local(queries, key_states, value_states, passing_rows):
    me = lax.axis_index("seq")
    z, h, c = me // 4, (me // 2) % 2, me % 2
    move = functools.partial(lax.ppermute, axis_name="seq")

    def flags(*conditions):
        return jnp.stack([jnp.asarray(x).astype(jnp.int32) for x in conditions])

    kv_heads = key_states.shape[1] // HD
    rows = key_states.shape[0]
    by_head = [
        x.reshape(rows, kv_heads, HD).transpose(1, 0, 2) for x in (key_states, value_states)
    ]
    parts = lax.all_to_all(
        jnp.stack(by_head, axis=1), "head", split_axis=0, concat_axis=0, tiled=True
    )
    mine, kv = select(mark(passing_rows), parts)
    peer = move(mine, perm=PEER)
    low, high = kv[:HALF], kv[HALF : 2 * HALF]
    halves = [
        move(half, perm=[(0, block)]) for block, half in ((1, high), (2, low), (3, high))
    ]
    pair = join(flags(me), mine, peer, kv, halves)
    one = move(pair, perm=ahead(1))
    three = move(pair, perm=ahead(3))

    def both(i):
        return ((i, 0, 2 * PASS), (i + 1, 0, 2 * PASS))

    def anchor(i):
        return ((i, 2 * PASS, 2 * PASS + HALF), (i + 1, 2 * PASS, 2 * PASS + HALF))

    arrays = [pair] + [None] * 7
    near = ((0, ((0, PASS, 2 * PASS),), GROUP),)
    fresh = ((1, both(2), GROUP),)
    more = ((2, anchor(2), 1), (3, both(4) + anchor(4), GROUP))
    side = (
        (4, ((1, 0, 2 * PASS),), GROUP),
        (5, ((1, 0, PASS),), SIDE),
        (6, ((1, PASS, 2 * PASS),), SIDE),
    )
    side_more = ((7, anchor(0), 1),)
    last = ((8, both(6) + anchor(6), 4), (3, both(6), GROUP))
    use = flags(
        h == 1, z >= 1, z == 1, z == 3,
        (h == 1) & (c == 1), (h == 0) & (c == 1), (h == 1) & (c == 0),
        (z == 0) & (me > 0), z == 2, z == 0, h + c == 0, z < 2,
    )
    q = queries

    acc, token = first_part(use, q, kv, arrays[:1], near)
    (one,) = after((one,), token)
    (three,) = after((three,), token)
    arrays[1] = move(after((pair,), token)[0], perm=SIBLING)
    two = move(one, perm=ahead(1, 1))
    arrays[2], arrays[3] = one, move(one, perm=SIBLING)
    arrays[4], arrays[5] = three, move(three, perm=SIBLING)
    acc, token = stage(use, q, acc, arrays, fresh, more, 9, 9)
    (two,) = after((two,), token)
    arrays[6], arrays[7] = two, move(two, perm=SIBLING)
    acc, _ = stage(use, q, acc, arrays, side, side_more, 10, 2)
    return final(use, q, acc, kv, arrays, near + fresh + more + side + side_more, last, 11)


def solution(mesh):
    in_specs = (
        P("seq", "head"),
        P(("seq", "head"), None),
        P(("seq", "head"), None),
        P("head", "seq"),
    )
    return jax.shard_map(
        local, mesh=mesh, in_specs=in_specs, out_specs=P("seq", "head"), check_vma=False
    )
```

```python
import functools

import jax
import jax.numpy as jnp
from jax import lax
from jax.experimental import pallas as pl
from jax.experimental.pallas import tpu as pltpu
from jax.sharding import PartitionSpec as P

HD = 128
GROUP = 8
BLK = 512
PASS = 256
HALF = 128
SIDE = 8
SCALE = float(HD**-0.5 * 1.4426950408889634)
LOW, HIGH = 2.0**-80, 2.0**100
BF16, F32 = jnp.bfloat16, jnp.float32
NT = (((1,), (1,)), ((), ()))
VMEM_BYTES = 24 * 2**20
SMEM = pl.BlockSpec(memory_space=pltpu.SMEM)
VMEM = pl.BlockSpec(memory_space=pltpu.VMEM)


TOKEN = jax.ShapeDtypeStruct((8, HD), F32)


def cost(units):
    return pl.CostEstimate(
        flops=int(units * 2 * 2 * GROUP * BLK * 256 * 256),
        bytes_accessed=1 << 20,
        transcendentals=int(units * GROUP * BLK * 256),
    )


def params():
    return pltpu.CompilerParams(vmem_limit_bytes=VMEM_BYTES)


def columns(r):
    return slice(r * HD, (r + 1) * HD)


def select_kernel(rows_ref, kv_ref, out_ref):
    ids = lax.broadcasted_iota(jnp.int32, (BLK, PASS), 0)
    picked = jnp.where(ids == rows_ref[...], 1.0, 0.0).astype(BF16)
    out_ref[...] = lax.dot_general(
        picked, kv_ref[...], (((0,), (0,)), ((), ())), preferred_element_type=F32
    ).astype(BF16)


def select(rows, kv):
    return pl.pallas_call(
        select_kernel,
        out_shape=jax.ShapeDtypeStruct((PASS, 2 * HD), BF16),
        in_specs=[VMEM, VMEM],
        out_specs=VMEM,
        compiler_params=params(),
        name="select_rows",
    )(rows, kv)


def join_kernel(me_ref, mine_ref, peer_ref, kv_ref, *refs):
    halves, out_ref = refs[:-1], refs[-1]
    out_ref[:PASS] = mine_ref[...]
    out_ref[PASS : 2 * PASS] = peer_ref[...]
    out_ref[2 * PASS :] = kv_ref[:HALF]
    for block, half_ref in enumerate(halves):

        @pl.when(me_ref[0] == block + 1)
        def _():
            out_ref[2 * PASS :] = half_ref[...]


def join(me, mine, peer, kv, halves):
    return pl.pallas_call(
        join_kernel,
        out_shape=jax.ShapeDtypeStruct((2 * PASS + HALF, 2 * HD), BF16),
        in_specs=[SMEM] + [VMEM] * (3 + len(halves)),
        out_specs=VMEM,
        compiler_params=params(),
        name="join_rows",
    )(me, mine, peer, kv, *halves)


def powers(scores):
    return jnp.exp2(scores * SCALE).astype(BF16)


def first_kernel(groups, use_ref, q_ref, kv_ref, *refs):
    near_refs, (acc_ref, token_ref, keys_near, wide) = refs[:-4], refs[-4:]
    token_ref[...] = jnp.zeros_like(token_ref)
    wide[:BLK, :HD] = kv_ref[:, HD:]
    wide[:BLK, HD:] = jnp.ones((BLK, HD), BF16)
    half = BLK // 2
    rows = lax.broadcasted_iota(jnp.int32, (half, half), 0)
    cols = lax.broadcasted_iota(jnp.int32, (half, half), 1)
    causal = cols <= rows
    keys = kv_ref[:, :HD]

    for r in range(GROUP):
        q = q_ref[:, columns(r)]
        scores = lax.dot_general(q, keys[:half], NT, preferred_element_type=F32)
        first = powers(jnp.where(causal, scores[:half], -jnp.inf))
        second = powers(scores[half:])
        scores = lax.dot_general(q[half:], keys[half:], NT, preferred_element_type=F32)
        third = powers(jnp.where(causal, scores, -jnp.inf))
        acc_ref[r, :half] = jnp.dot(first, wide[:half], preferred_element_type=F32)
        acc_ref[r, half:] = jnp.dot(
            jnp.concatenate([second, third], axis=1), wide[:BLK], preferred_element_type=F32
        )

    def put(r, across, total):
        acc_ref[r] = total

    run_groups(groups, use_ref, q_ref, acc_ref, near_refs, keys_near, wide, put)


def first_part(use, q, kv, arrays, groups):
    rows = max(BLK, *[rows_of(case) for _, case, _ in groups])
    return pl.pallas_call(
        functools.partial(first_kernel, groups),
        out_shape=(jax.ShapeDtypeStruct((GROUP, BLK, 2 * HD), F32), TOKEN),
        in_specs=[SMEM] + [VMEM] * (2 + len(arrays)),
        out_specs=(VMEM, VMEM),
        scratch_shapes=[pltpu.VMEM((rows, HD), BF16), pltpu.VMEM((rows, 2 * HD), BF16)],
        compiler_params=params(),
        cost_estimate=cost(2.5),
        name="first_blocks",
    )(use, q, kv, *arrays)


def rows_of(case):
    return sum(stop - start for _, start, stop in case)


def heads(body, unroll):
    if unroll == GROUP:
        for r in range(GROUP):
            body(r, columns(r))
        return

    def step(r, carry):
        body(r, pl.ds(pl.multiple_of(r * HD, HD), HD))
        return carry

    lax.fori_loop(0, GROUP, step, 0, unroll=unroll)


def weighted(case, unroll, q_ref, acc_ref, kv_refs, keys, wide, put):
    at = 0
    for i, start, stop in case:
        end = at + stop - start
        keys[at:end] = kv_refs[i][start:stop, :HD]
        wide[at:end, :HD] = kv_refs[i][start:stop, HD:]
        wide[at:end, HD:] = jnp.ones((end - at, HD), BF16)
        at = end

    def body(r, across):
        scores = lax.dot_general(q_ref[:, across], keys[:at], NT, preferred_element_type=F32)
        put(r, across, acc_ref[r] + jnp.dot(powers(scores), wide[:at], preferred_element_type=F32))

    heads(body, unroll)


def run_groups(groups, use_ref, q_ref, acc_ref, kv_refs, keys, wide, put):
    for flag, case, unroll in groups:

        @pl.when(use_ref[flag] != 0)
        def _():
            weighted(case, unroll, q_ref, acc_ref, kv_refs, keys, wide, put)


def hand_over(use_ref, flag, acc_ref, put):
    @pl.when(use_ref[flag] != 0)
    def _():
        heads(lambda r, across: put(r, across, acc_ref[r]), 1)


def stage_kernel(fresh, more, idle, use_ref, q_ref, *refs):
    kv_refs, (acc_in, acc_ref, token_ref, keys, wide) = refs[:-5], refs[-5:]
    token_ref[...] = jnp.zeros_like(token_ref)

    def put(r, across, total):
        acc_ref[r] = total

    hand_over(use_ref, idle, acc_in, put)
    run_groups(fresh, use_ref, q_ref, acc_in, kv_refs, keys, wide, put)
    run_groups(more, use_ref, q_ref, acc_ref, kv_refs, keys, wide, put)


def stage(use, q, acc, arrays, fresh, more, idle, units):
    rows = max(rows_of(case) for _, case, _ in fresh + more)
    used = sorted({i for _, case, _ in fresh + more for i, _, _ in case})
    fresh, more = (
        [
            (flag, [(used.index(i), start, stop) for i, start, stop in case], unroll)
            for flag, case, unroll in groups
        ]
        for groups in (fresh, more)
    )
    return pl.pallas_call(
        functools.partial(stage_kernel, fresh, more, idle),
        out_shape=(jax.ShapeDtypeStruct(acc.shape, F32), TOKEN),
        in_specs=[SMEM] + [VMEM] * (2 + len(used)),
        out_specs=(VMEM, VMEM),
        scratch_shapes=[pltpu.VMEM((rows, HD), BF16), pltpu.VMEM((rows, 2 * HD), BF16)],
        compiler_params=params(),
        cost_estimate=cost(units),
        name="add_blocks",
    )(use, q, *[arrays[i] for i in used], acc)


def online(q, keys, values, usable, running):
    top, total, mixed = running
    scores = lax.dot_general(q, keys, NT, preferred_element_type=F32) * SCALE
    if usable is not None:
        scores = jnp.where(usable, scores, -jnp.inf)
    fresh = jnp.maximum(top, jnp.max(scores, axis=1, keepdims=True))
    rescale = jnp.exp2(top - fresh)
    weights = jnp.exp2(scores - fresh)
    total = total * rescale + jnp.sum(weights, axis=1, keepdims=True)
    mixed = mixed * rescale + jnp.dot(weights.astype(BF16), values, preferred_element_type=F32)
    return fresh, total, mixed


def final_kernel(earlier, last, idle, use_ref, q_ref, *refs):
    kv_refs, (local_ref, acc_in, result_ref, keys, wide, worst, out_ref, sems) = refs[:-8], refs[-8:]
    worst[...] = jnp.zeros_like(worst)

    def send(r, across):
        return pltpu.make_async_copy(
            out_ref.at[:, across], result_ref.at[:, across], sems.at[r]
        )

    def put(r, across, weighted_sum):
        total = weighted_sum[:, HD:]
        worst[...] = jnp.maximum(
            worst[...], jnp.where((total > LOW) & (total < HIGH), 0.0, 1.0)
        )
        out_ref[:, across] = (weighted_sum[:, :HD] / total).astype(BF16)
        send(r, across).start()

    hand_over(use_ref, idle, acc_in, put)
    run_groups(last, use_ref, q_ref, acc_in, kv_refs, keys, wide, put)

    for r in range(GROUP):
        send(r, columns(r)).wait()

    @pl.when(jnp.max(worst[...]) > 0.0)
    def _():
        tile = 128

        def redo(step, carry):
            r, t = step // (BLK // tile), step % (BLK // tile)
            here = pl.ds(pl.multiple_of(t * tile, tile), tile)
            across = pl.ds(pl.multiple_of(r * HD, HD), HD)
            q = q_ref[here, across]
            running = (
                jnp.full((tile, 1), -1e30, F32),
                jnp.zeros((tile, 1), F32),
                jnp.zeros((tile, HD), F32),
            )
            rows = t * tile + lax.broadcasted_iota(jnp.int32, (tile, BLK), 0)
            cols = lax.broadcasted_iota(jnp.int32, (tile, BLK), 1)
            running = online(q, local_ref[:, :HD], local_ref[:, HD:], cols <= rows, running)
            for flag, case, _ in earlier + last:

                def more(state, case=case):
                    for i, start, stop in case:
                        kv = kv_refs[i]
                        state = online(q, kv[start:stop, :HD], kv[start:stop, HD:], None, state)
                    return state

                running = lax.cond(use_ref[flag] != 0, more, lambda state: state, running)
            out_ref[here, across] = (running[2] / running[1]).astype(BF16)
            return carry

        lax.fori_loop(0, GROUP * (BLK // tile), redo, 0)
        pltpu.sync_copy(out_ref, result_ref)


def final(use, q, acc, local_kv, arrays, earlier, last, idle):
    rows = max(rows_of(case) for _, case, _ in last)
    return pl.pallas_call(
        functools.partial(final_kernel, earlier, last, idle),
        out_shape=jax.ShapeDtypeStruct((BLK, GROUP * HD), BF16),
        in_specs=[SMEM] + [VMEM] * (3 + len(arrays)),
        out_specs=pl.BlockSpec(memory_space=pl.ANY),
        scratch_shapes=[
            pltpu.VMEM((rows, HD), BF16),
            pltpu.VMEM((rows, 2 * HD), BF16),
            pltpu.VMEM((BLK, HD), F32),
            pltpu.VMEM((BLK, GROUP * HD), BF16),
            pltpu.SemaphoreType.DMA((GROUP,)),
        ],
        compiler_params=params(),
        cost_estimate=cost(4),
        name="last_blocks",
    )(use, q, *arrays, local_kv, acc)


SIBLING = [(s, s ^ 1) for s in range(16)]
PEER = [(s, s ^ 2) for s in range(16)]


def ahead(d, first=0):
    return [(s, s + 4 * d) for s in range(4 * first, 16 - 4 * d)]


def after(messages, token):
    def kernel(*refs):
        del refs

    return pl.pallas_call(
        kernel,
        out_shape=tuple(jax.ShapeDtypeStruct(x.shape, x.dtype) for x in messages),
        in_specs=[VMEM] * (len(messages) + 1),
        out_specs=(VMEM,) * len(messages),
        input_output_aliases={i: i for i in range(len(messages))},
        compiler_params=params(),
        name="hand_on",
    )(*messages, token)


def local(queries, key_states, value_states, passing_rows):
    me = lax.axis_index("seq")
    z, h, c = me // 4, (me // 2) % 2, me % 2
    move = functools.partial(lax.ppermute, axis_name="seq")

    def flags(*conditions):
        return jnp.stack([jnp.asarray(x).astype(jnp.int32) for x in conditions])

    kv_heads = key_states.shape[1] // HD
    rows = key_states.shape[0]
    both = jnp.concatenate(
        [key_states.reshape(rows, kv_heads, HD), value_states.reshape(rows, kv_heads, HD)], axis=2
    ).transpose(1, 0, 2)
    kv = lax.all_to_all(both, "head", split_axis=0, concat_axis=0, tiled=True).reshape(BLK, 2 * HD)

    mine = select(passing_rows, kv)
    peer = move(mine, perm=PEER)
    low, high = kv[:HALF], kv[HALF : 2 * HALF]
    halves = [
        move(half, perm=[(0, block)]) for block, half in ((1, high), (2, low), (3, high))
    ]
    pair = join(flags(me), mine, peer, kv, halves)
    one = move(pair, perm=ahead(1))
    three = move(pair, perm=ahead(3))

    def both(i):
        return ((i, 0, 2 * PASS), (i + 1, 0, 2 * PASS))

    def anchor(i):
        return ((i, 2 * PASS, 2 * PASS + HALF), (i + 1, 2 * PASS, 2 * PASS + HALF))

    arrays = [pair] + [None] * 7
    near = ((0, ((0, PASS, 2 * PASS),), GROUP),)
    fresh = ((1, both(2), GROUP),)
    more = ((2, anchor(2), 1), (3, both(4) + anchor(4), GROUP))
    side = (
        (4, ((1, 0, 2 * PASS),), GROUP),
        (5, ((1, 0, PASS),), SIDE),
        (6, ((1, PASS, 2 * PASS),), SIDE),
    )
    side_more = ((7, anchor(0), 1),)
    last = ((8, both(6) + anchor(6), 4), (3, both(6), GROUP))
    use = flags(
        h == 1, z >= 1, z == 1, z == 3,
        (h == 1) & (c == 1), (h == 0) & (c == 1), (h == 1) & (c == 0),
        (z == 0) & (me > 0), z == 2, z == 0, h + c == 0, z < 2,
    )
    q = queries

    acc, token = first_part(use, q, kv, arrays[:1], near)
    (one,) = after((one,), token)
    (three,) = after((three,), token)
    arrays[1] = move(after((pair,), token)[0], perm=SIBLING)
    two = move(one, perm=ahead(1, 1))
    arrays[2], arrays[3] = one, move(one, perm=SIBLING)
    arrays[4], arrays[5] = three, move(three, perm=SIBLING)
    acc, token = stage(use, q, acc, arrays, fresh, more, 9, 9)
    (two,) = after((two,), token)
    arrays[6], arrays[7] = two, move(two, perm=SIBLING)
    acc, _ = stage(use, q, acc, arrays, side, side_more, 10, 2)
    return final(use, q, acc, kv, arrays, near + fresh + more + side + side_more, last, 11)


def solution(mesh):
    in_specs = (
        P("seq", "head"),
        P(("seq", "head"), None),
        P(("seq", "head"), None),
        P("head", "seq"),
    )
    return jax.shard_map(
        local, mesh=mesh, in_specs=in_specs, out_specs=P("seq", "head"), check_vma=False
    )
```
